32 devices in a mesh: groups: 2 (over y), slab: 8 (over z, x), sub: 2 (over core).
Axes of the slice: x: 2, y: 2, z: 4, core: 2. Of those that a mesh axis runs over, the one named last changes fastest.
Arguments:
- fingerprints: bfloat16 [16384, 2048], P(('groups', 'slab', 'sub')), parts along dimension 0, may hold values from 0 to 30, as said below
- coefficients: bfloat16 [16384, 128], P(('groups', 'slab', 'sub')), parts along dimension 0, may hold values from -1.5 to 1.5
- counts: int32 [16], P('groups'), parts along dimension 0, may hold values from 1 to 1024, 6144 in all
- families: int32 [16], P('groups'), parts along dimension 0, may hold values from 0 to 3, never falling along the last dimension, each value on 1 to 3 neighbouring positions
Outputs:
- kernel_product: float32 [16384, 128], P(('groups', 'slab', 'sub')), parts along dimension 0
The draws below stay inside these ranges and needn't reach their ends.
There are 2 independent parts, one for each index of `groups`. The reference program is written for one: setup_inputs(seed, part) draws one part's arguments, and reference() takes and returns one part's arrays. A program takes and returns all parts, laid end to end along the dimension named above; each array names one. Nothing has to cross between parts.
Inputs may be any that keep to these rules, and one draw needn't show every extreme that they name: `counts`: every live pose of a slab comes before its padding slots, and some slab is full. `families`: family ids never fall from one slab to the next, a family spans at most 3 slabs, and some family spans exactly that many. `fingerprints`: entries are non-negative and every fingerprint has a positive entry.
All inputs are finite; a program needn't handle non-finite values.
Results may differ from the reference program's by a relative error of at most 0.0003.
Values may be sent and summed in bfloat16 or wider, within the bound.
A program may use at most 64 MiB of HBM per device.

```python
import math
import jax
import jax.numpy as jnp
import numpy as np
from jax import lax

SLAB = 1024
F = 2048
ASSAYS = 128
MOST_SLABS = 3
NSLABS = 8
POSES = 8192
FAMILIES = 4
LIVE_POSES = 6144


def draw_fingerprints(key, part):
    key = jax.random.fold_in(key, 11)
    key_mask, key_size = jax.random.split(key, 2)
    live_mask = jax.random.bernoulli(key_mask, 0.4, (POSES, F))
    row_ids = lax.broadcasted_iota(jnp.int32, (POSES, F), 0)
    col_ids = lax.broadcasted_iota(jnp.int32, (POSES, F), 1)
    live_mask = jnp.logical_or(live_mask, col_ids == row_ids % F)
    magnitude = jax.random.uniform(key_size, (POSES, F), jnp.float32, 0.5, 2.0)
    return jnp.where(live_mask, magnitude, 0.0).astype(jnp.bfloat16)


def shard_levels(rng, dims, cuts, smallest, top_value):
    loudness, own = 1.0, jax.random.fold_in(rng, 6)
    for dim, blocks in cuts:
        heights = jnp.exp(jax.random.uniform(jax.random.fold_in(own, dim), (blocks,), jnp.float32, smallest / len(cuts), top_value / len(cuts)))
        loudness = loudness * jnp.repeat(heights, dims[dim] // blocks).reshape([-1 if axis == dim else 1 for axis in range(len(dims))])
    return loudness


def split_up(count, total, reach, slope):
    weights = [(1 << 20) // math.isqrt(grade ** slope) + 1 for grade in range(2, count + 1)]
    spare, given = total - reach - (count - 1), [1] * (count - 1)
    while spare > 0:
        candidates = [i for i in range(count - 1) if given[i] < reach]
        whole, budget = sum([weights[i] for i in candidates]), spare
        for i in candidates:
            addition = min(reach - given[i], max(1, budget * weights[i] // whole), spare)
            given[i] = given[i] + addition
            spare = spare - addition
    return np.array([reach] + given)


def uneven_parts(own_key, number_of, total, most, skew):
    if number_of == 2:
        one = jax.random.randint(own_key, (), max(1, total - most), min(most, total - 1) + 1)
        return jnp.stack([one, total - one])
    tallies = jnp.asarray(split_up(number_of, total, most, skew), jnp.int32)
    couples = (number_of - 1) // 2
    source_of, receiver = tallies[1:1 + 2 * couples:2], tallies[2:2 + 2 * couples:2]
    room = jnp.minimum(source_of - 1, most - receiver)
    moved = jax.random.randint(jax.random.fold_in(own_key, 1), (couples,), 0, 1 << 20) % (room + 1)
    tallies = tallies.at[1:1 + 2 * couples:2].set(source_of - moved).at[2:2 + 2 * couples:2].set(receiver + moved)
    return tallies[jax.random.permutation(jax.random.fold_in(own_key, 2), number_of)]


def normal_values(stream_key, dims, deviation, most, cuts=(), kind=jnp.bfloat16):
    array = deviation * jax.random.normal(stream_key, dims, jnp.float32)
    if cuts:
        array = array * shard_levels(stream_key, dims, cuts, -0.22, 0.18)
    return jnp.clip(array, -most, most).astype(kind)


def setup_inputs(seed: int = 0, part: int = 0) -> dict:
    streams_of = jax.random.split(jax.random.key(seed), 5)
    part_keys = jax.random.split(jax.random.fold_in(streams_of[4], part), 5)
    return {
        "fingerprints": draw_fingerprints(jax.random.fold_in(jax.random.fold_in(streams_of[4], part), 71), part),
        "coefficients": normal_values(part_keys[1], (POSES, ASSAYS), 0.25, 1.5, ((0, 16),)),
        "counts": uneven_parts(part_keys[2], NSLABS, LIVE_POSES, SLAB, 1).astype(jnp.int32),
        "families": jnp.searchsorted(jnp.cumsum(uneven_parts(part_keys[3], FAMILIES, NSLABS, MOST_SLABS, 0)), jnp.arange(NSLABS), side="right").astype(jnp.int32),
    }


ridge_weight = 0.5


def tanimoto(row_prints, col_prints, row_norms, col_norms):
    gram_tile = jnp.dot(row_prints, col_prints.T, precision=lax.Precision.HIGHEST)
    return gram_tile / (row_norms[:, None] + col_norms[None, :] - gram_tile)


def block_norms(block_prints):
    return jnp.sum(jnp.square(block_prints.astype(jnp.float32)), axis=1)


def reference(fingerprints, coefficients, counts, families):
    slab_prints = fingerprints.reshape(NSLABS, SLAB, F)
    coeff_slabs = coefficients.astype(jnp.float32).reshape(NSLABS, SLAB, ASSAYS)
    position = jnp.arange(SLAB, dtype=jnp.int32)
    validity = (position[None, :] < counts[:, None]).astype(jnp.float32)
    squared_norms = lax.map(block_norms, slab_prints)
    slab_ids = jnp.arange(NSLABS, dtype=jnp.int32)
    accumulated = ridge_weight * coeff_slabs
    for offset in range(MOST_SLABS):
        def pair_tile(row_slab):
            col_slab = jnp.minimum(row_slab + offset, NSLABS - 1).astype(jnp.int32)
            present = jnp.logical_and(row_slab + offset < NSLABS, families[col_slab] == families[row_slab]).astype(jnp.float32)
            kernel = tanimoto(slab_prints[row_slab].astype(jnp.float32), slab_prints[col_slab].astype(jnp.float32), squared_norms[row_slab], squared_norms[col_slab])
            kernel = kernel * (present * validity[row_slab])[:, None] * validity[col_slab][None, :]
            forward_part = jnp.dot(kernel, coeff_slabs[col_slab], precision=lax.Precision.HIGHEST)
            backward_part = jnp.dot(kernel.T, coeff_slabs[row_slab], precision=lax.Precision.HIGHEST)
            return forward_part, backward_part
        forward_part, backward_part = lax.map(pair_tile, slab_ids)
        accumulated = accumulated + forward_part
        if offset > 0:
            accumulated = accumulated + jnp.roll(backward_part, offset, axis=0)
    return (accumulated * validity[:, :, None]).reshape(POSES, ASSAYS)
```

```python
import functools

import jax
import jax.numpy as jnp
from jax import lax
from jax.experimental import pallas as pl
from jax.experimental.pallas import tpu as pltpu
from jax.sharding import PartitionSpec as P

STEPS = 4
ridge_weight = 0.5
MESH = pl.DeviceIdType.MESH


def kernel(
    slab_count, feat, prints, coeffs, counts, families, out,
    ob, xb, zb, acc, accz, ret, ocol, zcol, orow, xrow, zrow,
    lsem, osem, xsem, zsem, fxsem, fzsem, rsem,
):
    half = coeffs.shape[0]
    size = half // STEPS
    tile = 2 * size
    s, c = lax.axis_index("slab"), lax.axis_index("sub")
    step_dir = 1 - 2 * lax.rem(s, 2)
    mate = 1 - c
    xs = s + step_dir
    src, dst = s + 2 * step_dir, s - 2 * step_dir
    has_src = jnp.logical_and(src >= 0, src < slab_count)
    has_dst = jnp.logical_and(dst >= 0, dst < slab_count)
    src_at, dst_at = jnp.clip(src, 0, slab_count - 1), jnp.clip(dst, 0, slab_count - 1)

    def own_rows(k):
        return pl.ds(pl.multiple_of(c * half + k * size, 16), size)

    def put_rows(k):
        return pl.ds(pl.multiple_of(k * tile + c * size, 16), size)

    def local(k):
        return pltpu.make_async_copy(
            prints.at[pl.ds(k * size, size), :], ob.at[own_rows(k), pl.ds(0, feat)], lsem.at[k]
        )

    def remote(source, target, sem, k, slab, sub):
        return pltpu.make_async_remote_copy(
            src_ref=source, dst_ref=target, send_sem=sem.at[0, k], recv_sem=sem.at[1, k],
            device_id={"slab": slab, "sub": sub}, device_id_type=MESH,
        )

    def x_copy(k):
        return remote(ob.at[own_rows(k), :], xb.at[put_rows(k), :], xsem, k, xs, c)

    def z_copy(k):
        return remote(ob.at[own_rows(k), :], zb.at[put_rows(k), :], zsem, k, dst_at, c)

    def x_pass(k):
        return remote(xb.at[put_rows(k), :], xb.at[put_rows(k), :], fxsem, k, s, mate)

    def z_pass(k):
        return remote(zb.at[put_rows(k), :], zb.at[put_rows(k), :], fzsem, k, s, mate)

    def o_copy():
        rows = pl.ds(pl.multiple_of(c * half, 16), half)
        return remote(ob.at[rows, :], ob.at[rows, :], osem, 0, s, mate)

    def ret_copy(k):
        rows = pl.ds(k * size, size)
        return remote(accz.at[rows, :], ret.at[rows, :], rsem, k, src_at, c)

    for k in range(STEPS):
        local(k).start()
    barrier = pltpu.get_barrier_semaphore()

    def greet(slab, sub):
        pl.semaphore_signal(
            barrier, inc=1, device_id={"slab": slab, "sub": sub}, device_id_type=MESH
        )

    greet(s, mate)
    greet(xs, c)
    pl.when(has_src)(lambda: greet(src_at, c))
    pl.when(has_dst)(lambda: greet(dst_at, c))

    place = c * half + lax.broadcasted_iota(jnp.int32, coeffs.shape, 0)
    live = place < counts[s]
    weights = jnp.where(live, coeffs[...].astype(jnp.float32), 0.0)
    ob[pl.ds(pl.multiple_of(c * half, 16), half), pl.ds(feat, coeffs.shape[1])] = weights.astype(
        jnp.bfloat16
    )
    pl.semaphore_wait(barrier, 2 + has_src.astype(jnp.int32) + has_dst.astype(jnp.int32))
    for k in range(STEPS):
        local(k).wait()
        x_copy(k).start()
        pl.when(has_dst)(lambda k=k: z_copy(k).start())
    o_copy().start()

    one, zero = jnp.float32(1), jnp.float32(0)
    own_family, x_family, z_family = families[s], families[xs], families[src_at]
    with_x = jnp.where(own_family == x_family, one, zero)
    with_z = jnp.where(own_family == z_family, one, zero)
    x_with_z = jnp.where(x_family == z_family, one, zero)

    def norms(buf, start, count):
        block = buf[pl.ds(start, count), pl.ds(0, feat)].astype(jnp.float32)
        return jnp.sum(block * block, axis=1, keepdims=True)

    def store_row(ref, j, values):
        wide = jnp.broadcast_to(values, (values.shape[0], 128))
        ref[j] = jnp.transpose(wide)[:8, :]

    def piece(rbuf, start, count, col, cbuf, j, row, flag, total, at):
        first = pl.multiple_of(j * tile, 16)
        gram = lax.dot_general(
            rbuf[pl.ds(start, count), pl.ds(0, feat)],
            cbuf[pl.ds(first, tile), pl.ds(0, feat)],
            (((1,), (1,)), ((), ())),
            preferred_element_type=jnp.float32,
        )
        values = gram / (col[pl.ds(at, count), :] + row[j][:1, :] - gram)
        high = values.astype(jnp.bfloat16)
        low = (values - high.astype(jnp.float32)).astype(jnp.bfloat16)
        col_weights = cbuf[pl.ds(first, tile), pl.ds(feat, coeffs.shape[1])]
        part = jnp.dot(high, col_weights, preferred_element_type=jnp.float32)
        part += jnp.dot(low, col_weights, preferred_element_type=jnp.float32)
        total[pl.ds(at, count), :] += part * flag

    def own_by(cbuf, j, row, flag):
        @pl.loop(0, half // tile)
        def _(i):
            at = pl.multiple_of(i * tile, 16)
            piece(ob, pl.multiple_of(c * half + at, 16), tile, ocol, cbuf, j, row, flag, acc, at)

    def z_by(i, cbuf, j, row, flag):
        start = pl.multiple_of(i * tile + c * size, 16)
        piece(zb, start, size, zcol, cbuf, j, row, flag, accz, pl.multiple_of(i * size, 16))

    acc[...] = weights * ridge_weight
    accz[...] = jnp.zeros_like(accz)

    @pl.loop(0, half // tile)
    def _(i):
        at = pl.multiple_of(i * tile, 16)
        ocol[pl.ds(at, tile), :] = norms(ob, pl.multiple_of(c * half + at, 16), tile)

    o_copy().wait_recv()

    @pl.loop(0, 2 * half // tile)
    def _(j):
        store_row(orow, j, norms(ob, pl.multiple_of(j * tile, 16), tile))
        own_by(ob, j, orow, one)

    for k in range(STEPS):
        last = k == STEPS - 1
        x_copy(k).wait_recv()
        x_pass(k).start()

        @pl.when(has_src)
        def _(k=k):
            z_copy(k).wait_recv()
            z_pass(k).start()
            zcol[pl.ds(k * size, size), :] = norms(
                zb, pl.multiple_of(k * tile + c * size, 16), size
            )

            @pl.loop(0, 2 * half // tile)
            def _(j):
                z_by(k, ob, j, orow, with_z)

        x_pass(k).wait_recv()
        store_row(xrow, k, norms(xb, k * tile, tile))

        @pl.when(has_src)
        def _(k=k, last=last):
            for i in range(k):
                z_by(i, xb, k, xrow, x_with_z)
                if last:
                    ret_copy(i).start()

            @pl.loop(0, k + 1)
            def _(j):
                z_by(k, xb, j, xrow, x_with_z)

            if last:
                ret_copy(k).start()
            z_pass(k).wait_recv()
            store_row(zrow, k, norms(zb, k * tile, tile))
            own_by(zb, k, zrow, with_z)

        own_by(xb, k, xrow, with_x)


    @pl.when(has_dst)
    def _():
        for k in range(STEPS):
            ret_copy(k).wait_recv()
        out[...] = jnp.where(live, acc[...] + ret[...], 0.0)

    @pl.when(jnp.logical_not(has_dst))
    def _():
        out[...] = jnp.where(live, acc[...], 0.0)

    o_copy().wait_send()
    for k in range(STEPS):
        x_copy(k).wait_send()
        x_pass(k).wait_send()

        @pl.when(has_dst)
        def _(k=k):
            z_copy(k).wait_send()

        @pl.when(has_src)
        def _(k=k):
            z_pass(k).wait_send()
            ret_copy(k).wait_send()


def body(fingerprints, coefficients, counts, families):
    half, feat = fingerprints.shape
    assays = coefficients.shape[1]
    slab_count = lax.axis_size("slab")
    size = half // STEPS
    tile = 2 * size
    tiles = 2 * half // tile
    bf16, f32 = jnp.bfloat16, jnp.float32
    pair = pltpu.SemaphoreType.DMA((2, STEPS))
    return pl.pallas_call(
        functools.partial(kernel, slab_count, feat),
        out_shape=jax.ShapeDtypeStruct((half, assays), f32),
        in_specs=[
            pl.BlockSpec(memory_space=pl.ANY),
            pl.BlockSpec(memory_space=pltpu.VMEM),
            pl.BlockSpec(memory_space=pltpu.SMEM),
            pl.BlockSpec(memory_space=pltpu.SMEM),
        ],
        out_specs=pl.BlockSpec(memory_space=pltpu.VMEM),
        scratch_shapes=[
            pltpu.VMEM((2 * half, feat + assays), bf16),
            pltpu.VMEM((2 * half, feat + assays), bf16),
            pltpu.VMEM((2 * half, feat + assays), bf16),
            pltpu.VMEM((half, assays), f32),
            pltpu.VMEM((half, assays), f32),
            pltpu.VMEM((half, assays), f32),
            pltpu.VMEM((half, 1), f32),
            pltpu.VMEM((half, 1), f32),
            pltpu.VMEM((tiles, 8, tile), f32),
            pltpu.VMEM((tiles, 8, tile), f32),
            pltpu.VMEM((tiles, 8, tile), f32),
            pltpu.SemaphoreType.DMA((STEPS,)),
            pltpu.SemaphoreType.DMA((2, 1)),
            pair, pair, pair, pair, pair,
        ],
        compiler_params=pltpu.CompilerParams(
            collective_id=0, has_side_effects=True, vmem_limit_bytes=48 * 1024 * 1024
        ),
        cost_estimate=pl.CostEstimate(
            flops=20 * half * half * feat, bytes_accessed=2 * half * feat, transcendentals=0
        ),
    )(fingerprints, coefficients, counts, families)


def solution(mesh):
    in_specs = (
        P(("groups", "slab", "sub"), None),
        P(("groups", "slab", "sub"), None),
        P("groups"),
        P("groups"),
    )
    out_specs = P(("groups", "slab", "sub"), None)
    return jax.shard_map(body, mesh=mesh, in_specs=in_specs, out_specs=out_specs, check_vma=False)
```

```python
import functools

import jax
import jax.numpy as jnp
from jax import lax
from jax.experimental import pallas as pl
from jax.experimental.pallas import tpu as pltpu
from jax.sharding import PartitionSpec as P

STEPS = 2
ridge_weight = 0.5
MESH = pl.DeviceIdType.MESH


def kernel(
    slab_count, feat, prints, coeffs_in, counts_in, families_in, out,
    ob, xb, zb, acc, accz, ret, ocol, zcol, orow, xrow, zrow,
    coeffs, counts, families, lsem, ssem, osem, xsem, zsem, fxsem, fzsem, rsem,
):
    half = coeffs.shape[0]
    size = half // STEPS
    tile = 2 * size
    s, c = lax.axis_index("slab"), lax.axis_index("sub")
    step_dir = 1 - 2 * lax.rem(s, 2)
    mate = 1 - c
    xs = s + step_dir
    src, dst = s + 2 * step_dir, s - 2 * step_dir
    has_src = jnp.logical_and(src >= 0, src < slab_count)
    has_dst = jnp.logical_and(dst >= 0, dst < slab_count)
    src_at, dst_at = jnp.clip(src, 0, slab_count - 1), jnp.clip(dst, 0, slab_count - 1)

    def own_rows(k):
        return pl.ds(pl.multiple_of(c * half + k * size, 16), size)

    def put_rows(k):
        return pl.ds(pl.multiple_of(k * tile + c * size, 16), size)

    def local(k):
        return pltpu.make_async_copy(
            prints.at[pl.ds(k * size, size), :], ob.at[own_rows(k), pl.ds(0, feat)], lsem.at[k]
        )

    def remote(source, target, sem, k, slab, sub):
        return pltpu.make_async_remote_copy(
            src_ref=source, dst_ref=target, send_sem=sem.at[0, k], recv_sem=sem.at[1, k],
            device_id={"slab": slab, "sub": sub}, device_id_type=MESH,
        )

    def x_copy(k):
        return remote(ob.at[own_rows(k), :], xb.at[put_rows(k), :], xsem, k, xs, c)

    def z_copy(k):
        return remote(ob.at[own_rows(k), :], zb.at[put_rows(k), :], zsem, k, dst_at, c)

    def x_pass(k):
        return remote(xb.at[put_rows(k), :], xb.at[put_rows(k), :], fxsem, k, s, mate)

    def z_pass(k):
        return remote(zb.at[put_rows(k), :], zb.at[put_rows(k), :], fzsem, k, s, mate)

    def o_copy():
        rows = pl.ds(pl.multiple_of(c * half, 16), half)
        return remote(ob.at[rows, :], ob.at[rows, :], osem, 0, s, mate)

    def ret_copy(k):
        rows = pl.ds(k * size, size)
        return remote(accz.at[rows, :], ret.at[rows, :], rsem, k, src_at, c)

    small = [
        pltpu.make_async_copy(source, target, ssem.at[i])
        for i, (source, target) in enumerate(
            ((coeffs_in, coeffs), (counts_in, counts), (families_in, families))
        )
    ]
    for copy in small:
        copy.start()
    for k in range(STEPS):
        local(k).start()
    barrier = pltpu.get_barrier_semaphore()

    def greet(slab, sub):
        pl.semaphore_signal(
            barrier, inc=1, device_id={"slab": slab, "sub": sub}, device_id_type=MESH
        )

    greet(s, mate)
    greet(xs, c)
    pl.when(has_src)(lambda: greet(src_at, c))
    pl.when(has_dst)(lambda: greet(dst_at, c))

    for copy in small:
        copy.wait()
    place = c * half + lax.broadcasted_iota(jnp.int32, coeffs.shape, 0)
    live = place < counts[s]
    weights = jnp.where(live, coeffs[...].astype(jnp.float32), 0.0)
    ob[pl.ds(pl.multiple_of(c * half, 16), half), pl.ds(feat, coeffs.shape[1])] = weights.astype(
        jnp.bfloat16
    )
    pl.semaphore_wait(barrier, 2 + has_src.astype(jnp.int32) + has_dst.astype(jnp.int32))
    for k in range(STEPS):
        local(k).wait()
        x_copy(k).start()
        pl.when(has_dst)(lambda k=k: z_copy(k).start())
    o_copy().start()

    one, zero = jnp.float32(1), jnp.float32(0)
    own_family, x_family, z_family = families[s], families[xs], families[src_at]
    with_x = jnp.where(own_family == x_family, one, zero)
    with_z = jnp.where(own_family == z_family, one, zero)
    x_with_z = jnp.where(x_family == z_family, one, zero)

    def norms(buf, start, count):
        block = buf[pl.ds(start, count), pl.ds(0, feat)].astype(jnp.float32)
        return jnp.sum(block * block, axis=1, keepdims=True)

    def store_row(ref, j, values):
        wide = jnp.broadcast_to(values, (values.shape[0], 128))
        ref[j] = jnp.transpose(wide)[:8, :]

    def piece(rbuf, start, count, col, cbuf, j, row, flag, total, at):
        first = pl.multiple_of(j * tile, 16)
        gram = lax.dot_general(
            rbuf[pl.ds(start, count), pl.ds(0, feat)],
            cbuf[pl.ds(first, tile), pl.ds(0, feat)],
            (((1,), (1,)), ((), ())),
            preferred_element_type=jnp.float32,
        )
        values = gram / (col[pl.ds(at, count), :] + row[j][:1, :] - gram)
        high = values.astype(jnp.bfloat16)
        low = (values - high.astype(jnp.float32)).astype(jnp.bfloat16)
        col_weights = cbuf[pl.ds(first, tile), pl.ds(feat, coeffs.shape[1])]
        part = jnp.dot(high, col_weights, preferred_element_type=jnp.float32)
        part += jnp.dot(low, col_weights, preferred_element_type=jnp.float32)
        total[pl.ds(at, count), :] += part * flag

    def own_by(cbuf, j, row, flag):
        @pl.loop(0, half // tile)
        def _(i):
            at = pl.multiple_of(i * tile, 16)
            piece(ob, pl.multiple_of(c * half + at, 16), tile, ocol, cbuf, j, row, flag, acc, at)

    def z_by(i, cbuf, j, row, flag):
        start = pl.multiple_of(i * tile + c * size, 16)
        piece(zb, start, size, zcol, cbuf, j, row, flag, accz, pl.multiple_of(i * size, 16))

    acc[...] = weights * ridge_weight
    accz[...] = jnp.zeros_like(accz)

    @pl.loop(0, half // tile)
    def _(i):
        at = pl.multiple_of(i * tile, 16)
        ocol[pl.ds(at, tile), :] = norms(ob, pl.multiple_of(c * half + at, 16), tile)

    o_copy().wait_recv()

    @pl.loop(0, 2 * half // tile)
    def _(j):
        store_row(orow, j, norms(ob, pl.multiple_of(j * tile, 16), tile))
        own_by(ob, j, orow, one)

    for k in range(STEPS):
        last = k == STEPS - 1
        x_copy(k).wait_recv()
        x_pass(k).start()

        @pl.when(has_src)
        def _(k=k):
            z_copy(k).wait_recv()
            z_pass(k).start()
            zcol[pl.ds(k * size, size), :] = norms(
                zb, pl.multiple_of(k * tile + c * size, 16), size
            )

            @pl.loop(0, 2 * half // tile)
            def _(j):
                z_by(k, ob, j, orow, with_z)

        x_pass(k).wait_recv()
        store_row(xrow, k, norms(xb, k * tile, tile))

        @pl.when(has_src)
        def _(k=k, last=last):
            for i in range(k):
                z_by(i, xb, k, xrow, x_with_z)
                if last:
                    ret_copy(i).start()

            @pl.loop(0, k + 1)
            def _(j):
                z_by(k, xb, j, xrow, x_with_z)

            if last:
                ret_copy(k).start()
            z_pass(k).wait_recv()
            store_row(zrow, k, norms(zb, k * tile, tile))
            own_by(zb, k, zrow, with_z)

        own_by(xb, k, xrow, with_x)


    @pl.when(has_dst)
    def _():
        for k in range(STEPS):
            ret_copy(k).wait_recv()
        out[...] = jnp.where(live, acc[...] + ret[...], 0.0)

    @pl.when(jnp.logical_not(has_dst))
    def _():
        out[...] = jnp.where(live, acc[...], 0.0)

    o_copy().wait_send()
    for k in range(STEPS):
        x_copy(k).wait_send()
        x_pass(k).wait_send()

        @pl.when(has_dst)
        def _(k=k):
            z_copy(k).wait_send()

        @pl.when(has_src)
        def _(k=k):
            z_pass(k).wait_send()
            ret_copy(k).wait_send()


def body(fingerprints, coefficients, counts, families):
    half, feat = fingerprints.shape
    assays = coefficients.shape[1]
    slab_count = lax.axis_size("slab")
    size = half // STEPS
    tile = 2 * size
    tiles = 2 * half // tile
    bf16, f32 = jnp.bfloat16, jnp.float32
    pair = pltpu.SemaphoreType.DMA((2, STEPS))
    return pl.pallas_call(
        functools.partial(kernel, slab_count, feat),
        out_shape=jax.ShapeDtypeStruct((half, assays), f32),
        in_specs=[
            pl.BlockSpec(memory_space=pltpu.HBM),
            pl.BlockSpec(memory_space=pltpu.HBM),
            pl.BlockSpec(memory_space=pltpu.HBM),
            pl.BlockSpec(memory_space=pltpu.HBM),
        ],
        out_specs=pl.BlockSpec(memory_space=pltpu.VMEM),
        scratch_shapes=[
            pltpu.VMEM((2 * half, feat + assays), bf16),
            pltpu.VMEM((2 * half, feat + assays), bf16),
            pltpu.VMEM((2 * half, feat + assays), bf16),
            pltpu.VMEM((half, assays), f32),
            pltpu.VMEM((half, assays), f32),
            pltpu.VMEM((half, assays), f32),
            pltpu.VMEM((half, 1), f32),
            pltpu.VMEM((half, 1), f32),
            pltpu.VMEM((tiles, 8, tile), f32),
            pltpu.VMEM((tiles, 8, tile), f32),
            pltpu.VMEM((tiles, 8, tile), f32),
            pltpu.VMEM((half, assays), bf16),
            pltpu.SMEM(counts.shape, jnp.int32),
            pltpu.SMEM(families.shape, jnp.int32),
            pltpu.SemaphoreType.DMA((STEPS,)),
            pltpu.SemaphoreType.DMA((3,)),
            pltpu.SemaphoreType.DMA((2, 1)),
            pair, pair, pair, pair, pair,
        ],
        compiler_params=pltpu.CompilerParams(
            collective_id=0, has_side_effects=True, vmem_limit_bytes=48 * 1024 * 1024
        ),
        cost_estimate=pl.CostEstimate(
            flops=20 * half * half * feat, bytes_accessed=2 * half * feat, transcendentals=0
        ),
    )(fingerprints, coefficients, counts, families)


def solution(mesh):
    in_specs = (
        P(("groups", "slab", "sub"), None),
        P(("groups", "slab", "sub"), None),
        P("groups"),
        P("groups"),
    )
    out_specs = P(("groups", "slab", "sub"), None)
    return jax.shard_map(body, mesh=mesh, in_specs=in_specs, out_specs=out_specs, check_vma=False)
```

```python
import functools

import jax
import jax.numpy as jnp
from jax import lax
from jax.experimental import pallas as pl
from jax.experimental.pallas import tpu as pltpu
from jax.sharding import PartitionSpec as P

STEPS = 2
ridge_weight = 0.5
MESH = pl.DeviceIdType.MESH


def kernel(
    slab_count, feat, prints, coeffs_in, counts_in, families_in, out,
    ob, xb, zb, acc, accz, ret, ocol, zcol, orow, xrow, zrow,
    coeffs, counts, families, lsem, ssem, osem, xsem, zsem, fxsem, fzsem, rsem,
):
    half = coeffs.shape[0]
    size = half // STEPS
    tile = 2 * size
    s, c = lax.axis_index("slab"), lax.axis_index("sub")
    step_dir = 1 - 2 * lax.rem(s, 2)
    mate = 1 - c
    xs = s + step_dir
    src, dst = s + 2 * step_dir, s - 2 * step_dir
    has_src = jnp.logical_and(src >= 0, src < slab_count)
    has_dst = jnp.logical_and(dst >= 0, dst < slab_count)
    src_at, dst_at = jnp.clip(src, 0, slab_count - 1), jnp.clip(dst, 0, slab_count - 1)

    def own_rows(k):
        return pl.ds(pl.multiple_of(c * half + k * size, 16), size)

    def put_rows(k):
        return pl.ds(pl.multiple_of(k * tile + c * size, 16), size)

    def local(k):
        return pltpu.make_async_copy(
            prints.at[pl.ds(k * size, size), :], ob.at[own_rows(k), pl.ds(0, feat)], lsem.at[k]
        )

    def remote(source, target, sem, k, slab, sub):
        return pltpu.make_async_remote_copy(
            src_ref=source, dst_ref=target, send_sem=sem.at[0, k], recv_sem=sem.at[1, k],
            device_id={"slab": slab, "sub": sub}, device_id_type=MESH,
        )

    def x_copy(k):
        return remote(ob.at[own_rows(k), :], xb.at[put_rows(k), :], xsem, k, xs, c)

    def z_copy(k):
        return remote(ob.at[own_rows(k), :], zb.at[put_rows(k), :], zsem, k, dst_at, c)

    def x_pass(k):
        return remote(xb.at[put_rows(k), :], xb.at[put_rows(k), :], fxsem, k, s, mate)

    def z_pass(k):
        return remote(zb.at[put_rows(k), :], zb.at[put_rows(k), :], fzsem, k, s, mate)

    def o_copy():
        rows = pl.ds(pl.multiple_of(c * half, 16), half)
        return remote(ob.at[rows, :], ob.at[rows, :], osem, 0, s, mate)

    def ret_copy(k):
        rows = pl.ds(k * size, size)
        return remote(accz.at[rows, :], ret.at[rows, :], rsem, k, src_at, c)

    small = [
        pltpu.make_async_copy(source, target, ssem.at[i])
        for i, (source, target) in enumerate(
            ((coeffs_in, coeffs), (counts_in, counts), (families_in, families))
        )
    ]
    for copy in small:
        copy.start()
    for k in range(STEPS):
        local(k).start()
    barrier = pltpu.get_barrier_semaphore()

    def greet(slab, sub):
        pl.semaphore_signal(
            barrier, inc=1, device_id={"slab": slab, "sub": sub}, device_id_type=MESH
        )

    greet(s, mate)
    greet(xs, c)
    pl.when(has_src)(lambda: greet(src_at, c))
    pl.when(has_dst)(lambda: greet(dst_at, c))

    for copy in small:
        copy.wait()
    place = c * half + lax.broadcasted_iota(jnp.int32, coeffs.shape, 0)
    live = place < counts[s]
    weights = jnp.where(live, coeffs[...].astype(jnp.float32), 0.0)
    ob[pl.ds(pl.multiple_of(c * half, 16), half), pl.ds(feat, coeffs.shape[1])] = weights.astype(
        jnp.bfloat16
    )
    pl.semaphore_wait(barrier, 2 + has_src.astype(jnp.int32) + has_dst.astype(jnp.int32))
    for k in range(STEPS):
        local(k).wait()
        x_copy(k).start()
        pl.when(has_dst)(lambda k=k: z_copy(k).start())
    o_copy().start()

    one, zero = jnp.float32(1), jnp.float32(0)
    own_family, x_family, z_family = families[s], families[xs], families[src_at]
    with_x = jnp.where(own_family == x_family, one, zero)
    with_z = jnp.where(own_family == z_family, one, zero)
    x_with_z = jnp.where(x_family == z_family, one, zero)

    def norms(buf, start, count):
        block = buf[pl.ds(start, count), pl.ds(0, feat)].astype(jnp.float32)
        return jnp.sum(block * block, axis=1, keepdims=True)

    def store_row(ref, j, values):
        wide = jnp.broadcast_to(values, (values.shape[0], 128))
        ref[j] = jnp.transpose(wide)[:8, :]

    def piece(rbuf, start, count, col, cbuf, j, row, flag, total, at):
        first = pl.multiple_of(j * tile, 16)
        gram = lax.dot_general(
            rbuf[pl.ds(start, count), pl.ds(0, feat)],
            cbuf[pl.ds(first, tile), pl.ds(0, feat)],
            (((1,), (1,)), ((), ())),
            preferred_element_type=jnp.float32,
        )
        values = gram / (col[pl.ds(at, count), :] + row[j][:1, :] - gram)
        high = values.astype(jnp.bfloat16)
        low = (values - high.astype(jnp.float32)).astype(jnp.bfloat16)
        col_weights = cbuf[pl.ds(first, tile), pl.ds(feat, coeffs.shape[1])]
        part = jnp.dot(high, col_weights, preferred_element_type=jnp.float32)
        part += jnp.dot(low, col_weights, preferred_element_type=jnp.float32)
        total[pl.ds(at, count), :] += part * flag

    def own_by(cbuf, j, row, flag):
        @pl.loop(0, half // tile)
        def _(i):
            at = pl.multiple_of(i * tile, 16)
            piece(ob, pl.multiple_of(c * half + at, 16), tile, ocol, cbuf, j, row, flag, acc, at)

    def z_by(i, cbuf, j, row, flag):
        start = pl.multiple_of(i * tile + c * size, 16)
        piece(zb, start, size, zcol, cbuf, j, row, flag, accz, pl.multiple_of(i * size, 16))

    acc[...] = weights * ridge_weight
    accz[...] = jnp.zeros_like(accz)

    @pl.loop(0, half // tile)
    def _(i):
        at = pl.multiple_of(i * tile, 16)
        ocol[pl.ds(at, tile), :] = norms(ob, pl.multiple_of(c * half + at, 16), tile)

    o_copy().wait_recv()

    @pl.loop(0, 2 * half // tile)
    def _(j):
        store_row(orow, j, norms(ob, pl.multiple_of(j * tile, 16), tile))
        own_by(ob, j, orow, one)

    for k in range(STEPS):
        last = k == STEPS - 1
        x_copy(k).wait_recv()
        x_pass(k).start()

        @pl.when(has_src)
        def _(k=k):
            z_copy(k).wait_recv()
            z_pass(k).start()
            zcol[pl.ds(k * size, size), :] = norms(
                zb, pl.multiple_of(k * tile + c * size, 16), size
            )

            @pl.loop(0, 2 * half // tile)
            def _(j):
                z_by(k, ob, j, orow, with_z)

            for j in range(k):
                z_by(k, xb, j, xrow, x_with_z)

        x_pass(k).wait_recv()
        store_row(xrow, k, norms(xb, k * tile, tile))

        @pl.when(has_src)
        def _(k=k, last=last):
            for i in range(k):
                z_by(i, xb, k, xrow, x_with_z)
                if last:
                    ret_copy(i).start()

            z_by(k, xb, k, xrow, x_with_z)
            if last:
                ret_copy(k).start()
            z_pass(k).wait_recv()
            store_row(zrow, k, norms(zb, k * tile, tile))
            own_by(zb, k, zrow, with_z)

        own_by(xb, k, xrow, with_x)


    @pl.when(has_dst)
    def _():
        for k in range(STEPS):
            ret_copy(k).wait_recv()
        out[...] = jnp.where(live, acc[...] + ret[...], 0.0)

    @pl.when(jnp.logical_not(has_dst))
    def _():
        out[...] = jnp.where(live, acc[...], 0.0)

    o_copy().wait_send()
    for k in range(STEPS):
        x_copy(k).wait_send()
        x_pass(k).wait_send()

        @pl.when(has_dst)
        def _(k=k):
            z_copy(k).wait_send()

        @pl.when(has_src)
        def _(k=k):
            z_pass(k).wait_send()
            ret_copy(k).wait_send()


def body(fingerprints, coefficients, counts, families):
    half, feat = fingerprints.shape
    assays = coefficients.shape[1]
    slab_count = lax.axis_size("slab")
    size = half // STEPS
    tile = 2 * size
    tiles = 2 * half // tile
    bf16, f32 = jnp.bfloat16, jnp.float32
    pair = pltpu.SemaphoreType.DMA((2, STEPS))
    return pl.pallas_call(
        functools.partial(kernel, slab_count, feat),
        out_shape=jax.ShapeDtypeStruct((half, assays), f32),
        in_specs=[
            pl.BlockSpec(memory_space=pltpu.HBM),
            pl.BlockSpec(memory_space=pltpu.HBM),
            pl.BlockSpec(memory_space=pltpu.HBM),
            pl.BlockSpec(memory_space=pltpu.HBM),
        ],
        out_specs=pl.BlockSpec(memory_space=pltpu.VMEM),
        scratch_shapes=[
            pltpu.VMEM((2 * half, feat + assays), bf16),
            pltpu.VMEM((2 * half, feat + assays), bf16),
            pltpu.VMEM((2 * half, feat + assays), bf16),
            pltpu.VMEM((half, assays), f32),
            pltpu.VMEM((half, assays), f32),
            pltpu.VMEM((half, assays), f32),
            pltpu.VMEM((half, 1), f32),
            pltpu.VMEM((half, 1), f32),
            pltpu.VMEM((tiles, 8, tile), f32),
            pltpu.VMEM((tiles, 8, tile), f32),
            pltpu.VMEM((tiles, 8, tile), f32),
            pltpu.VMEM((half, assays), bf16),
            pltpu.SMEM(counts.shape, jnp.int32),
            pltpu.SMEM(families.shape, jnp.int32),
            pltpu.SemaphoreType.DMA((STEPS,)),
            pltpu.SemaphoreType.DMA((3,)),
            pltpu.SemaphoreType.DMA((2, 1)),
            pair, pair, pair, pair, pair,
        ],
        compiler_params=pltpu.CompilerParams(
            collective_id=0, has_side_effects=True, vmem_limit_bytes=48 * 1024 * 1024
        ),
        cost_estimate=pl.CostEstimate(
            flops=20 * half * half * feat, bytes_accessed=2 * half * feat, transcendentals=0
        ),
    )(fingerprints, coefficients, counts, families)


def solution(mesh):
    in_specs = (
        P(("groups", "slab", "sub"), None),
        P(("groups", "slab", "sub"), None),
        P("groups"),
        P("groups"),
    )
    out_specs = P(("groups", "slab", "sub"), None)
    return jax.shard_map(body, mesh=mesh, in_specs=in_specs, out_specs=out_specs, check_vma=False)
```
